256 devices in a mesh: tok: 8 (over x, core), code: 32 (over y, z).
Axes of the slice: x: 4, y: 4, z: 8, core: 2. Of those that a mesh axis runs over, the one named last changes fastest.
Arguments:
- latents: bfloat16 [2048, 256], P('tok'), may hold values from -240 to 240
- codebook: bfloat16 [262144, 256], P('code'), may hold values from -1.1953125 to 1.1953125
- cotangent: bfloat16 [2048, 256], P('tok'), may hold values from -6 to 6
- chosen: int32 [2048], P('tok'), may hold values from 0 to 262143
Outputs:
- latent_grad: float32 [2048, 256], P('tok')
- code_grad: float32 [262144, 256], P(('code', 'tok'))
The draws below stay inside these ranges and needn't reach their ends.
All inputs are finite; a program needn't handle non-finite values.
Results may differ from the reference program's by a relative error of at most 0.004.
Values may be sent and summed in bfloat16 or wider, within the bound.
A program may use at most 64 MiB of HBM per device.

```python
import jax
import jax.numpy as jnp
from jax import lax

D = 256
CODE_DEV = 8192
TOKENS = 2048
CODES = 262144


def draw_latents(key, part):
    key = jax.random.fold_in(key, 11)
    values = jnp.clip(jax.random.normal(key, (TOKENS, D), jnp.float32), -6.0, 6.0)
    return values.astype(jnp.bfloat16)


def set_ends(values, own_key, low, largest):
    dims = values.shape
    index_at = [jax.random.randint(jax.random.fold_in(own_key, axis), (), 0, dims[axis]) for axis in range(len(dims))]
    values = values.at[tuple(index_at)].set(low)
    longest = dims.index(max(dims))
    index_at[longest] = (index_at[longest] + 1) % dims[longest]
    return values.at[tuple(index_at)].set(largest)


def shard_levels(rng, dims, split, smallest, top_value):
    def one(position, shards_of):
        steps = jax.random.uniform(jax.random.fold_in(jax.random.fold_in(rng, 6), position), (shards_of,), jnp.float32, smallest / len(split), top_value / len(split))
        return jnp.repeat(jnp.exp(steps), dims[position] // shards_of).reshape((-1,) + (1,) * (len(dims) - position - 1))

    level = one(*split[0])
    for cut in split[1:]:
        level = level * one(*cut)
    return level


def gaussian(key, dims, scale, limit, split=(), held_as=jnp.bfloat16):
    entries = scale * jax.random.normal(key, dims, jnp.float32)
    if split:
        entries = entries * shard_levels(key, dims, split, -0.22, 0.18)
    return jnp.clip(entries, -limit, limit).astype(held_as)


def setup_inputs(seed: int = 0) -> dict:
    streams_of = jax.random.split(jax.random.key(seed), 5)
    return {
        "latents": draw_latents(jax.random.fold_in(streams_of[4], 71), 0),
        "codebook": gaussian(streams_of[1], (CODES, D), 0.1875, 1.1953125, ((0, 32),)),
        "cotangent": gaussian(streams_of[2], (TOKENS, D), 1.0, 6.0, ((0, 8),)),
        "chosen": set_ends(jax.random.randint(streams_of[3], (TOKENS,), 0, CODES), jax.random.fold_in(streams_of[3], 1), 0, CODES - 1).astype(jnp.int32),
    }


def reference(latents, codebook, cotangent, chosen):
    tok_rows = latents.shape[0]
    width = latents.shape[1]
    code_rows = codebook.shape[0]
    block = min(2048, CODE_DEV)
    count = code_rows // block
    blocks = codebook.reshape(count, block, width)
    columns = lax.iota(jnp.int32, block)

    def stats_step(carry, part):
        top, total = carry
        scores = jnp.dot(latents, part.T, preferred_element_type=jnp.float32)
        newtop = jnp.maximum(top, jnp.max(scores, axis=1))
        total = total * jnp.exp(top - newtop) + jnp.sum(jnp.exp(scores - newtop[:, None]), axis=1)
        return (newtop, total), None

    start_top = jnp.full((tok_rows,), -1e30, jnp.float32)
    (top, total), unused = lax.scan(stats_step, (start_top, jnp.zeros((tok_rows,), jnp.float32)), blocks)

    def probs_of(part):
        scores = jnp.dot(latents, part.T, preferred_element_type=jnp.float32)
        return jnp.exp(scores - top[:, None]) / total[:, None]

    def inner_step(carry, part):
        upstream = jnp.dot(cotangent, part.T, preferred_element_type=jnp.float32)
        return carry + jnp.sum(probs_of(part) * upstream, axis=1), None

    inner, unused = lax.scan(inner_step, jnp.zeros((tok_rows,), jnp.float32), blocks)

    def grad_step(carry, item):
        part, index = item
        upstream = jnp.dot(cotangent, part.T, preferred_element_type=jnp.float32)
        dlogits = (probs_of(part) * (upstream - inner[:, None])).astype(jnp.bfloat16)
        carry = carry + jnp.dot(dlogits, part, preferred_element_type=jnp.float32)
        ids = (index * block + columns).astype(jnp.int32)
        onehot = (chosen.astype(jnp.int32)[:, None] == ids[None, :]).astype(jnp.bfloat16)
        grads = jnp.dot(dlogits.T, latents, preferred_element_type=jnp.float32)
        grads = grads + jnp.dot(onehot.T, cotangent, preferred_element_type=jnp.float32)
        return carry, grads

    indices = lax.iota(jnp.int32, count)
    latent_grad, code_parts = lax.scan(grad_step, jnp.zeros((tok_rows, width), jnp.float32), (blocks, indices))
    return latent_grad, code_parts.reshape(code_rows, width)
```

```python
import jax
import jax.numpy as jnp
from jax import lax
from jax.experimental import pallas as pl
from jax.experimental.pallas import tpu as pltpu
from jax.sharding import PartitionSpec as P

MESH = pl.DeviceIdType.MESH
F32, BF16 = jnp.float32, jnp.bfloat16
NX, NY, NZ = 4, 4, 8
PLANE = NY * NZ
T = 256
D = 256
CODES = 8192
OWN = CODES // NX
HALF = OWN // 2
ROWS = 256

SHIFTS = sorted(
    ((dy, dz) for dy in range(NY) for dz in range(NZ) if (dy, dz) != (0, 0)),
    key=lambda s: -(min(s[0], NY - s[0]) + min(s[1], NZ - s[1])),
)
LOG2E = 1.4426950408889634
PARTS = (2048, 2048, 4096)
STEP = 1024


def nt(a, b):
    return lax.dot_general(a, b, (((1,), (1,)), ((), ())), preferred_element_type=F32)


def tn(a, b):
    return lax.dot_general(a, b, (((0,), (0,)), ((), ())), preferred_element_type=F32)


def nn(a, b):
    return jnp.dot(a, b, preferred_element_type=F32)


def row(v):
    return jnp.concatenate([v[0:1], v[1:2]], axis=1)


def pair(v):
    return jnp.concatenate([v[:, :128], v[:, 128:]], axis=0)


def fold8(v):
    return v.reshape(v.shape[0] // 8, 8, v.shape[1])


def rank_of(y, z):
    late = jnp.where(z < 5, z, jnp.where(z == 7, 5, z + 1))
    return late * NY + y


def code_of(rank):
    y, late = rank & (NY - 1), rank >> 2
    z = jnp.where(late < 5, late, jnp.where(late == 5, 7, late - 1))
    return y * NZ + z


def kernel(
    lat_hbm, cot_hbm, cho_hbm, cb_hbm, ag, cg_out,
    cb, lat, cot, cho, lq, uu, lb, ub, stats, fin, acc_a, acc_b,
    rs_out, rs_in, ag_own, cacc, cx_out, cx_in, cg,
    cb_sem, own_sem, gat_send, gat_recv, st_send, st_recv, fin_send, fin_recv,
    rs_send, rs_recv, ag_send, ag_recv, cx_send, cx_recv, out_sem, ready_sem,
):
    tok, code = lax.axis_index("tok"), lax.axis_index("code")
    x, c = tok >> 1, tok & 1
    y, z = code >> 3, code & (NZ - 1)

    x_peers = [((((x + d) & (NX - 1)) << 1) + c, code) for d in range(1, NX)]
    plane_codes = [(((y + dy) & (NY - 1)) << 3) + ((z + dz) & (NZ - 1)) for dy, dz in SHIFTS]
    plane = [(tok, p) for p in plane_codes]
    other = (tok ^ 1, code)

    def remote(src, dst, send, recv, to):
        return pltpu.make_async_remote_copy(
            src_ref=src, dst_ref=dst, send_sem=send, recv_sem=recv, device_id=to, device_id_type=MESH
        )

    def all_of(ref, send, recv):
        return remote(ref, ref, send, recv, other)

    own = [
        pltpu.make_async_copy(lat_hbm, lat.at[0], own_sem.at[0]),
        pltpu.make_async_copy(cot_hbm, cot.at[0], own_sem.at[1]),
        pltpu.make_async_copy(cho_hbm, cho.at[0], own_sem.at[2]),
    ]
    starts = [sum(PARTS[:k]) for k in range(len(PARTS))]
    loads = [
        pltpu.make_async_copy(cb_hbm.at[pl.ds(at, n)], cb.at[pl.ds(at, n)], cb_sem.at[k])
        for k, (at, n) in enumerate(zip(starts, PARTS))
    ]
    own[0].start()
    for load in loads:
        load.start()
    own[1].start()
    own[2].start()

    rank = rank_of(y, z)

    def tell(sem):
        def one(r, carry):
            pl.semaphore_signal(sem, inc=1, device_id=(tok, code_of(r)), device_id_type=MESH)
            return carry

        return one

    with jax.named_scope("greet"):
        barrier = pltpu.get_barrier_semaphore()
        near = x_peers + [other]
        for p in near:
            pl.semaphore_signal(barrier, inc=1, device_id=p, device_id_type=MESH)
        lax.fori_loop(rank + 1, PLANE, tell(barrier), 0)

    def logits(k, top):
        rows = pl.ds(starts[k], PARTS[k])
        loads[k].wait()
        scores = nt(cb[rows, :], lat[0]) * LOG2E
        lq[rows, :] = scores
        return jnp.maximum(top, jnp.max(fold8(scores), axis=0))

    with jax.named_scope("own_wait"):
        own[0].wait()
    with jax.named_scope("logits_first"):
        top8 = logits(0, jnp.full((8, T), -jnp.inf, F32))

    with jax.named_scope("entry"):
        pl.semaphore_wait(barrier, len(near) + rank)
    for d in (2, 1, 3):
        to = x_peers[d - 1]
        remote(lat_hbm, lat.at[d], gat_send.at[0], gat_recv.at[0], to).start()
        remote(cot_hbm, cot.at[d], gat_send.at[1], gat_recv.at[1], to).start()
        remote(cho_hbm, cho.at[d], gat_send.at[2], gat_recv.at[2], to).start()
    lax.fori_loop(0, rank, tell(ready_sem), 0)

    with jax.named_scope("logits_rest"):
        for k in range(1, len(PARTS)):
            top8 = logits(k, top8)
        top = jnp.max(top8, axis=0, keepdims=True)
        own[1].wait()
        own[2].wait()

    with jax.named_scope("stats"):

        def stats_step(k, carry):
            total8, inner8 = carry
            rows = pl.ds(pl.multiple_of(k * STEP, STEP), STEP)
            up = nt(cb[rows, :], cot[0])
            uu[rows, :] = up
            q = jnp.exp2(lq[rows, :] - top)
            lq[rows, :] = q
            total8 = total8 + jnp.sum(fold8(q), axis=0)
            inner8 = inner8 + jnp.sum(fold8(q * up), axis=0)
            return total8, inner8

        zero8 = jnp.zeros((8, T), F32)
        total8, inner8 = lax.fori_loop(0, CODES // STEP, stats_step, (zero8, zero8), unroll=True)
        total = jnp.sum(total8, axis=0, keepdims=True)
        inner = jnp.sum(inner8, axis=0, keepdims=True)
        stats[0, 0] = pair(top)
        stats[0, 1] = pair(total)
        stats[0, 2] = pair(inner)
    with jax.named_scope("ready"):

        @pl.when(rank < PLANE - 1)
        def later_ones():
            pl.semaphore_wait(ready_sem, PLANE - 1 - rank)

    for k, p in enumerate(plane):
        remote(stats.at[0], stats.at[k + 1], st_send, st_recv, p).start()
    inner_loc = inner / total

    with jax.named_scope("sums"):
        acc_a[...] = jnp.zeros_like(acc_a)
        acc_b[...] = jnp.zeros_like(acc_b)

        def sums_step(k, carry):
            rows = pl.ds(pl.multiple_of(k * STEP, STEP), STEP)
            q = lq[rows, :]
            part = cb[rows, :]
            acc_a[...] += tn(part, (q * (uu[rows, :] - inner_loc)).astype(BF16))
            acc_b[...] += tn(part, q.astype(BF16))
            return carry

        lax.fori_loop(0, CODES // STEP, sums_step, 0, unroll=True)

    with jax.named_scope("stats_wait"):
        all_of(stats.at[pl.ds(1, PLANE - 1)], st_send, st_recv).wait_recv()
    with jax.named_scope("combine"):
        tops = stats[:, 0]
        big = jnp.max(tops, axis=0)
        weights = jnp.exp2(tops - big)
        whole = jnp.sum(weights * stats[:, 1], axis=0)
        scale = 1.0 / whole
        mean = jnp.sum(weights * stats[:, 2], axis=0) * scale
        fin[0, 0] = big
        fin[0, 1] = scale
        fin[0, 2] = mean
        own_scale = row(jnp.exp2(pair(top) - big) * scale)
        own_inner = row(mean)
        part = own_scale * (acc_a[...] - (own_inner - inner_loc) * acc_b[...])
        rs_out[...] = jnp.concatenate(
            [part[:, :128].reshape(PLANE, 8, 128), part[:, 128:].reshape(PLANE, 8, 128)], axis=1
        ).astype(BF16)
    for k, p in enumerate(plane):
        remote(rs_out.at[plane_codes[k]], rs_in.at[k], rs_send, rs_recv, p).start()
    for d in (2, 1, 3):
        remote(fin.at[0], fin.at[d], fin_send, fin_recv, x_peers[d - 1]).start()

    base = pl.multiple_of(x * OWN, OWN)

    def scores_of_codes():
        with jax.named_scope("gather_wait"):
            all_of(lat.at[pl.ds(1, NX - 1)], gat_send.at[0], gat_recv.at[0]).wait_recv()
            all_of(cot.at[pl.ds(1, NX - 1)], gat_send.at[1], gat_recv.at[1]).wait_recv()
            all_of(cho.at[pl.ds(1, NX - 1)], gat_send.at[2], gat_recv.at[2]).wait_recv()
        with jax.named_scope("code_scores"):
            codes = pl.ds(base, OWN)
            for g in range(1, NX):
                lb[g - 1] = nt(cb[codes, :], lat[g]) * LOG2E
                ub[g - 1] = nt(cb[codes, :], cot[g])
        with jax.named_scope("chosen"):
            ids = lax.broadcasted_iota(jnp.int32, (ROWS, T), 0)
            all_cot = cot[...].reshape(NX * T, D)

            def chosen_step(k, carry):
                at = pl.multiple_of(k * ROWS, ROWS)
                first = code * CODES + base + at
                hot = [jnp.where(ids == cho[g] - first, 1.0, 0.0).astype(BF16) for g in range(NX)]
                cacc[pl.ds(at, ROWS), :] = nn(jnp.concatenate(hot, axis=1), all_cot)
                return carry

            lax.fori_loop(0, OWN // ROWS, chosen_step, 0, unroll=True)

    pl.when(z < NZ // 2)(scores_of_codes)

    with jax.named_scope("rs_wait"):
        all_of(rs_in, rs_send, rs_recv).wait_recv()
    with jax.named_scope("latent_sum"):
        mine = rs_out[code].astype(F32) + jnp.sum(rs_in[...].astype(F32), axis=0)
        ag_own[...] = mine.astype(BF16)
    for p in plane:
        remote(ag_own, ag.at[code], ag_send, ag_recv, p).start()
    ag_local = pltpu.make_async_copy(ag_own, ag.at[code], out_sem.at[1])
    ag_local.start()

    pl.when(z >= NZ // 2)(scores_of_codes)

    with jax.named_scope("fin_wait"):
        all_of(fin.at[pl.ds(1, NX - 1)], fin_send, fin_recv).wait_recv()

    with jax.named_scope("code_grads"):
        bigs = [row(fin[g, 0]) for g in range(NX)]
        scales = [row(fin[g, 1]) for g in range(NX)]
        means = [row(fin[g, 2]) for g in range(NX)]
        all_lat = lat[...].reshape(NX * T, D)

        def grads_of(half, k):
            at = pl.multiple_of(half * HALF + k * ROWS, ROWS)
            rows = pl.ds(at, ROWS)
            own_rows = pl.ds(pl.multiple_of(base + at, ROWS), ROWS)
            dlogits = [((lq[own_rows, :] * own_scale) * (uu[own_rows, :] - own_inner)).astype(BF16)]
            for g in range(1, NX):
                probs = jnp.exp2(lb[g - 1, rows, :] - bigs[g]) * scales[g]
                dlogits.append((probs * (ub[g - 1, rows, :] - means[g])).astype(BF16))
            return cacc[rows, :] + nn(jnp.concatenate(dlogits, axis=1), all_lat)

        def other_step(k, carry):
            cx_out[pl.ds(pl.multiple_of(k * ROWS, ROWS), ROWS), :] = grads_of(1 - c, k).astype(BF16)
            return carry

        lax.fori_loop(0, HALF // ROWS, other_step, 0, unroll=True)
        to_other = remote(cx_out, cx_in, cx_send, cx_recv, other)
        to_other.start()

        def own_step(k, carry):
            cg[pl.ds(pl.multiple_of(k * ROWS, ROWS), ROWS), :] = grads_of(c, k)
            return carry

        lax.fori_loop(0, HALF // ROWS, own_step, 0, unroll=True)

    with jax.named_scope("core_wait"):
        to_other.wait_recv()
    with jax.named_scope("code_out"):
        cg[...] += cx_in[...].astype(F32)
        out_cg = pltpu.make_async_copy(cg, cg_out, out_sem.at[0])
        out_cg.start()

    with jax.named_scope("drain"):
        to_other.wait_send()
        all_of(lat.at[pl.ds(1, NX - 1)], gat_send.at[0], gat_recv.at[0]).wait_send()
        all_of(cot.at[pl.ds(1, NX - 1)], gat_send.at[1], gat_recv.at[1]).wait_send()
        all_of(cho.at[pl.ds(1, NX - 1)], gat_send.at[2], gat_recv.at[2]).wait_send()
        all_of(stats.at[pl.ds(1, PLANE - 1)], st_send, st_recv).wait_send()
        all_of(fin.at[pl.ds(1, NX - 1)], fin_send, fin_recv).wait_send()
        all_of(rs_in, rs_send, rs_recv).wait_send()
        ag_local.wait()
        out_cg.wait()

    with jax.named_scope("ag_wait"):
        all_of(rs_in, ag_send, ag_recv).wait_send()
        all_of(rs_in, ag_send, ag_recv).wait_recv()


def finish(ag, cg, lg_out, cg_out, ag_v, lg_v, cg_v, sem):
    load = pltpu.make_async_copy(ag, ag_v, sem.at[0])
    load.start()
    n = cg_v.shape[0]
    pieces = [pl.ds(k * (HALF // n), HALF // n) for k in range(n)]
    moves = [pltpu.make_async_copy(cg.at[p], cg_v.at[k], sem.at[2 + k]) for k, p in enumerate(pieces)]
    for move in moves:
        move.start()
    load.wait()
    full = ag_v[...].astype(F32)
    lg_v[pl.ds(0, 128), :] = full[:, :8, :].reshape(D, 128).T
    lg_v[pl.ds(128, 128), :] = full[:, 8:, :].reshape(D, 128).T
    store = pltpu.make_async_copy(lg_v, lg_out, sem.at[1])
    store.start()
    stores = [pltpu.make_async_copy(cg_v.at[k], cg_out.at[p], sem.at[2 + n + k]) for k, p in enumerate(pieces)]
    for move, out in zip(moves, stores):
        move.wait()
        out.start()
    store.wait()
    for out in stores:
        out.wait()


def shards(latents, codebook, cotangent, chosen):
    any_space = pl.BlockSpec(memory_space=pl.ANY)
    dma = pltpu.SemaphoreType.DMA
    gathered, code_grad = pl.pallas_call(
        kernel,
        out_shape=(
            jax.ShapeDtypeStruct((PLANE, 16, 128), BF16),
            jax.ShapeDtypeStruct((HALF, D), F32),
        ),
        in_specs=[any_space] * 4,
        out_specs=(any_space, any_space),
        scratch_shapes=[
            pltpu.VMEM((CODES, D), BF16),
            pltpu.VMEM((NX, T, D), BF16),
            pltpu.VMEM((NX, T, D), BF16),
            pltpu.VMEM((NX, 1, T), jnp.int32),
            pltpu.VMEM((CODES, T), F32),
            pltpu.VMEM((CODES, T), F32),
            pltpu.VMEM((NX - 1, OWN, T), F32),
            pltpu.VMEM((NX - 1, OWN, T), F32),
            pltpu.VMEM((PLANE, 3, 2, 128), F32),
            pltpu.VMEM((NX, 3, 2, 128), F32),
            pltpu.VMEM((D, T), F32),
            pltpu.VMEM((D, T), F32),
            pltpu.VMEM((PLANE, 16, 128), BF16),
            pltpu.VMEM((PLANE - 1, 16, 128), BF16),
            pltpu.VMEM((16, 128), BF16),
            pltpu.VMEM((OWN, D), F32),
            pltpu.VMEM((HALF, D), BF16),
            pltpu.VMEM((HALF, D), BF16),
            pltpu.VMEM((HALF, D), F32),
            dma((len(PARTS),)),
            dma((3,)),
            dma((3,)), dma((3,)),
            dma, dma,
            dma, dma,
            dma, dma,
            dma, dma,
            dma, dma,
            dma((2,)),
            pltpu.SemaphoreType.REGULAR,
        ],
        compiler_params=pltpu.CompilerParams(
            collective_id=0, has_side_effects=True, vmem_limit_bytes=56 * 2**20
        ),
        cost_estimate=pl.CostEstimate(
            flops=20 * T * D * CODES, bytes_accessed=8 * 2**20, transcendentals=2 * T * CODES
        ),
    )(latents, cotangent, chosen.reshape(1, T), codebook)
    return pl.pallas_call(
        finish,
        out_shape=(jax.ShapeDtypeStruct((T, D), F32), jax.ShapeDtypeStruct((HALF, D), F32)),
        in_specs=[any_space] * 2,
        out_specs=(any_space, any_space),
        scratch_shapes=[
            pltpu.VMEM((PLANE, 16, 128), BF16),
            pltpu.VMEM((T, D), F32),
            pltpu.VMEM((4, HALF // 4, D), F32),
            dma((10,)),
        ],
    )(gathered, code_grad)


def solution(mesh):
    in_specs = (P("tok", None), P("code", None), P("tok", None), P("tok"))
    out_specs = (P("tok", None), P(("code", "tok"), None))
    return jax.shard_map(shards, mesh=mesh, in_specs=in_specs, out_specs=out_specs, check_vma=False)
```

```python
import jax
import jax.numpy as jnp
from jax import lax
from jax.experimental import pallas as pl
from jax.experimental.pallas import tpu as pltpu
from jax.sharding import PartitionSpec as P

MESH = pl.DeviceIdType.MESH
F32, BF16 = jnp.float32, jnp.bfloat16
NX, NY, NZ = 4, 4, 8
PLANE = NY * NZ
T = 256
D = 256
CODES = 8192
OWN = CODES // NX
HALF = OWN // 2
ROWS = 256

SHIFTS = sorted(
    ((dy, dz) for dy in range(NY) for dz in range(NZ) if (dy, dz) != (0, 0)),
    key=lambda s: -(min(s[0], NY - s[0]) + min(s[1], NZ - s[1])),
)
LOG2E = 1.4426950408889634
PARTS = (1024, 3072, 4096)
STEP = 1024


def nt(a, b):
    return lax.dot_general(a, b, (((1,), (1,)), ((), ())), preferred_element_type=F32)


def tn(a, b):
    return lax.dot_general(a, b, (((0,), (0,)), ((), ())), preferred_element_type=F32)


def nn(a, b):
    return jnp.dot(a, b, preferred_element_type=F32)


def row(v):
    return jnp.concatenate([v[0:1], v[1:2]], axis=1)


def pair(v):
    return jnp.concatenate([v[:, :128], v[:, 128:]], axis=0)


def fold8(v):
    return v.reshape(v.shape[0] // 8, 8, v.shape[1])


def rank_of(y, z):
    late = jnp.where(z < 5, z, jnp.where(z == 7, 5, z + 1))
    return late * NY + y


def code_of(rank):
    y, late = rank & (NY - 1), rank >> 2
    z = jnp.where(late < 5, late, jnp.where(late == 5, 7, late - 1))
    return y * NZ + z


def kernel(
    lat_hbm, cot_hbm, cho_hbm, cb_hbm, ag, cg,
    cb, lat, cot, cho, lq, uu, lb, ub, stats, fin, acc_a, acc_b,
    rs_out, rs_in, coef, ag_own, cacc, cx_out, cx_in,
    cb_sem, own_sem, gat_send, gat_recv, st_send, st_recv, fin_send, fin_recv,
    rs_send, rs_recv, ag_send, ag_recv, cx_send, cx_recv, ready_sem,
):
    tok, code = lax.axis_index("tok"), lax.axis_index("code")
    x, c = tok >> 1, tok & 1
    y, z = code >> 3, code & (NZ - 1)

    x_peers = [((((x + d) & (NX - 1)) << 1) + c, code) for d in range(1, NX)]
    plane_codes = [(((y + dy) & (NY - 1)) << 3) + ((z + dz) & (NZ - 1)) for dy, dz in SHIFTS]
    plane = [(tok, p) for p in plane_codes]
    other = (tok ^ 1, code)

    def remote(src, dst, send, recv, to):
        return pltpu.make_async_remote_copy(
            src_ref=src, dst_ref=dst, send_sem=send, recv_sem=recv, device_id=to, device_id_type=MESH
        )

    def all_of(ref, send, recv):
        return remote(ref, ref, send, recv, other)

    own = [
        pltpu.make_async_copy(lat_hbm, lat.at[0], own_sem.at[0]),
        pltpu.make_async_copy(cot_hbm, cot.at[0], own_sem.at[1]),
        pltpu.make_async_copy(cho_hbm, cho.at[0], own_sem.at[2]),
    ]
    starts = [sum(PARTS[:k]) for k in range(len(PARTS))]
    loads = [
        pltpu.make_async_copy(cb_hbm.at[pl.ds(at, n)], cb.at[pl.ds(at, n)], cb_sem.at[k])
        for k, (at, n) in enumerate(zip(starts, PARTS))
    ]
    own[0].start()
    for load in loads:
        load.start()
    own[1].start()
    own[2].start()

    rank = rank_of(y, z)

    def tell(sem):
        def one(r, carry):
            pl.semaphore_signal(sem, inc=1, device_id=(tok, code_of(r)), device_id_type=MESH)
            return carry

        return one

    with jax.named_scope("greet"):
        barrier = pltpu.get_barrier_semaphore()
        near = x_peers + [other]
        for p in near:
            pl.semaphore_signal(barrier, inc=1, device_id=p, device_id_type=MESH)
        lax.fori_loop(rank + 1, PLANE, tell(barrier), 0)

    def logits(k, top):
        loads[k].wait()

        def step(j, top):
            rows = pl.ds(pl.multiple_of(starts[k] + j * STEP, STEP), STEP)
            scores = nt(cb[rows, :], lat[0]) * LOG2E
            lq[rows, :] = scores
            return jnp.maximum(top, jnp.max(fold8(scores), axis=0))

        return lax.fori_loop(0, PARTS[k] // STEP, step, top, unroll=True)

    with jax.named_scope("own_wait"):
        own[0].wait()
    with jax.named_scope("logits_first"):
        top8 = logits(0, jnp.full((8, T), -jnp.inf, F32))
        top8 = logits(1, top8)

    with jax.named_scope("entry"):
        pl.semaphore_wait(barrier, len(near) + rank)
    for d in (2, 1, 3):
        to = x_peers[d - 1]
        remote(lat_hbm, lat.at[d], gat_send.at[0], gat_recv.at[0], to).start()
        remote(cot_hbm, cot.at[d], gat_send.at[1], gat_recv.at[1], to).start()
        remote(cho_hbm, cho.at[d], gat_send.at[2], gat_recv.at[2], to).start()
    lax.fori_loop(0, rank, tell(ready_sem), 0)

    with jax.named_scope("logits_rest"):
        top8 = logits(2, top8)
        top = jnp.max(top8, axis=0, keepdims=True)
        own[1].wait()
        own[2].wait()

    with jax.named_scope("stats"):

        def stats_step(k, carry):
            total8, inner8 = carry
            rows = pl.ds(pl.multiple_of(k * STEP, STEP), STEP)
            up = nt(cb[rows, :], cot[0])
            uu[rows, :] = up
            q = jnp.exp2(lq[rows, :] - top)
            lq[rows, :] = q
            total8 = total8 + jnp.sum(fold8(q), axis=0)
            inner8 = inner8 + jnp.sum(fold8(q * up), axis=0)
            return total8, inner8

        zero8 = jnp.zeros((8, T), F32)
        total8, inner8 = lax.fori_loop(0, CODES // STEP, stats_step, (zero8, zero8), unroll=True)
        total = jnp.sum(total8, axis=0, keepdims=True)
        inner = jnp.sum(inner8, axis=0, keepdims=True)
        inner_loc = inner / total
        stats[0, 0] = pair(top + jnp.log(total) * LOG2E)
        stats[0, 1] = pair(inner_loc)

    def send_stats():
        with jax.named_scope("ready"):

            @pl.when(rank < PLANE - 1)
            def later_ones():
                pl.semaphore_wait(ready_sem, PLANE - 1 - rank)

        for k, p in enumerate(plane):
            remote(stats.at[0], stats.at[k + 1], st_send, st_recv, p).start()

    pl.when(z >= NZ // 2)(send_stats)

    with jax.named_scope("sums"):
        acc_a[...] = jnp.zeros_like(acc_a)
        acc_b[...] = jnp.zeros_like(acc_b)

        def sums_step(k, carry):
            rows = pl.ds(pl.multiple_of(k * STEP, STEP), STEP)
            q = lq[rows, :]
            part = cb[rows, :]
            acc_a[...] += tn(part, (q * (uu[rows, :] - inner_loc)).astype(BF16))
            acc_b[...] += tn(part, q.astype(BF16))
            return carry

        lax.fori_loop(0, CODES // STEP, sums_step, 0, unroll=True)

        for i, acc in enumerate((acc_a, acc_b)):
            whole = acc[...] * (1.0 / total)
            rs_out[:, i] = jnp.concatenate(
                [whole[:, :128].reshape(PLANE, 8, 128), whole[:, 128:].reshape(PLANE, 8, 128)], axis=1
            ).astype(BF16)
    pl.when(z < NZ // 2)(send_stats)
    for k, p in enumerate(plane):
        remote(rs_out.at[plane_codes[k]], rs_in.at[k + 1], rs_send, rs_recv, p).start()
    rs_local = pltpu.make_async_copy(rs_out.at[code], rs_in.at[0], own_sem.at[3])
    rs_local.start()

    with jax.named_scope("stats_wait"):
        all_of(stats.at[pl.ds(1, PLANE - 1)], st_send, st_recv).wait_recv()
    with jax.named_scope("combine"):
        logs = stats[:, 0]
        inners = stats[:, 1]
        big = jnp.max(logs, axis=0)
        weights = jnp.exp2(logs - big)
        whole = jnp.sum(weights, axis=0)
        weights = weights * (1.0 / whole)
        mean = jnp.sum(weights * inners, axis=0)
        fin[0, 0] = big + jnp.log(whole) * LOG2E
        fin[0, 1] = mean
        coef[:, 0] = weights
        coef[:, 1] = weights * (mean - inners)
        own_scale = row(weights[0]) * (1.0 / total)
        own_inner = row(mean)
    for d in (2, 1, 3):
        remote(fin.at[0], fin.at[d], fin_send, fin_recv, x_peers[d - 1]).start()

    base = pl.multiple_of(x * OWN, OWN)

    def scores_of_codes():
        with jax.named_scope("gather_wait"):
            all_of(lat.at[pl.ds(1, NX - 1)], gat_send.at[0], gat_recv.at[0]).wait_recv()
            all_of(cot.at[pl.ds(1, NX - 1)], gat_send.at[1], gat_recv.at[1]).wait_recv()
            all_of(cho.at[pl.ds(1, NX - 1)], gat_send.at[2], gat_recv.at[2]).wait_recv()
        with jax.named_scope("code_scores"):
            codes = pl.ds(base, OWN)
            for g in range(1, NX):
                lb[g - 1] = nt(cb[codes, :], lat[g]) * LOG2E
                ub[g - 1] = nt(cb[codes, :], cot[g])
        with jax.named_scope("chosen"):
            ids = lax.broadcasted_iota(jnp.int32, (ROWS, T), 0)
            all_cot = cot[...].reshape(NX * T, D)

            def chosen_step(k, carry):
                at = pl.multiple_of(k * ROWS, ROWS)
                first = code * CODES + base + at
                hot = [jnp.where(ids == cho[g] - first, 1.0, 0.0).astype(BF16) for g in range(NX)]
                cacc[pl.ds(at, ROWS), :] = nn(jnp.concatenate(hot, axis=1), all_cot)
                return carry

            lax.fori_loop(0, OWN // ROWS, chosen_step, 0, unroll=True)

    pl.when(z < NZ // 2 - 1)(scores_of_codes)

    with jax.named_scope("rs_wait"):
        rs_local.wait()
        all_of(rs_in.at[pl.ds(1, PLANE - 1)], rs_send, rs_recv).wait_recv()
    with jax.named_scope("latent_sum"):
        parts = rs_in[...].astype(F32).reshape(PLANE, 2, 2, 8, 128)
        by_a = coef[:, 0].reshape(PLANE, 2, 1, 128)
        by_b = coef[:, 1].reshape(PLANE, 2, 1, 128)
        mine = jnp.sum(by_a * parts[:, 0] - by_b * parts[:, 1], axis=0)
        ag_own[...] = mine.reshape(16, 128).astype(BF16)
        ag[code] = ag_own[...]

    def ag_to(r, carry):
        remote(ag_own, ag.at[code], ag_send, ag_recv, (tok, code_of(r))).start()
        return carry

    lax.fori_loop(0, rank, ag_to, 0)
    lax.fori_loop(rank + 1, PLANE, ag_to, 0)

    pl.when(z >= NZ // 2 - 1)(scores_of_codes)

    with jax.named_scope("fin_wait"):
        all_of(fin.at[pl.ds(1, NX - 1)], fin_send, fin_recv).wait_recv()

    with jax.named_scope("code_grads"):
        logs_of = [row(fin[g, 0]) for g in range(NX)]
        means = [row(fin[g, 1]) for g in range(NX)]
        all_lat = lat[...].reshape(NX * T, D)

        def grads_of(half, k):
            at = pl.multiple_of(half * HALF + k * ROWS, ROWS)
            rows = pl.ds(at, ROWS)
            own_rows = pl.ds(pl.multiple_of(base + at, ROWS), ROWS)
            dlogits = [((lq[own_rows, :] * own_scale) * (uu[own_rows, :] - own_inner)).astype(BF16)]
            for g in range(1, NX):
                probs = jnp.exp2(lb[g - 1, rows, :] - logs_of[g])
                dlogits.append((probs * (ub[g - 1, rows, :] - means[g])).astype(BF16))
            return cacc[rows, :] + nn(jnp.concatenate(dlogits, axis=1), all_lat)

        def other_step(k, carry):
            cx_out[pl.ds(pl.multiple_of(k * ROWS, ROWS), ROWS), :] = grads_of(1 - c, k).astype(BF16)
            return carry

        lax.fori_loop(0, HALF // ROWS, other_step, 0, unroll=True)
        to_other = remote(cx_out, cx_in, cx_send, cx_recv, other)
        to_other.start()

        def own_step(k, carry):
            cg[pl.ds(pl.multiple_of(k * ROWS, ROWS), ROWS), :] = grads_of(c, k)
            return carry

        lax.fori_loop(0, HALF // ROWS, own_step, 0, unroll=True)

    with jax.named_scope("core_wait"):
        to_other.wait_recv()
    with jax.named_scope("code_out"):
        cg[...] += cx_in[...].astype(F32)

    with jax.named_scope("drain"):
        to_other.wait_send()
        all_of(lat.at[pl.ds(1, NX - 1)], gat_send.at[0], gat_recv.at[0]).wait_send()
        all_of(cot.at[pl.ds(1, NX - 1)], gat_send.at[1], gat_recv.at[1]).wait_send()
        all_of(cho.at[pl.ds(1, NX - 1)], gat_send.at[2], gat_recv.at[2]).wait_send()
        all_of(stats.at[pl.ds(1, PLANE - 1)], st_send, st_recv).wait_send()
        all_of(fin.at[pl.ds(1, NX - 1)], fin_send, fin_recv).wait_send()
        all_of(rs_in.at[pl.ds(1, PLANE - 1)], rs_send, rs_recv).wait_send()

    with jax.named_scope("ag_wait"):
        all_of(ag.at[pl.ds(0, PLANE - 1)], ag_send, ag_recv).wait_send()
        all_of(ag.at[pl.ds(0, PLANE - 1)], ag_send, ag_recv).wait_recv()


def finish(ag, cg, lg_out, cg_out, lg_v, sem):
    move = pltpu.make_async_copy(cg, cg_out, sem.at[0])
    move.start()
    full = ag[...].astype(F32)
    lg_v[pl.ds(0, 128), :] = full[:, :8, :].reshape(D, 128).T
    lg_v[pl.ds(128, 128), :] = full[:, 8:, :].reshape(D, 128).T
    store = pltpu.make_async_copy(lg_v, lg_out, sem.at[1])
    store.start()
    with jax.named_scope("store_latent"):
        store.wait()
    with jax.named_scope("store_code"):
        move.wait()


def shards(latents, codebook, cotangent, chosen):
    any_space = pl.BlockSpec(memory_space=pl.ANY)
    vmem = pl.BlockSpec(memory_space=pltpu.VMEM)
    dma = pltpu.SemaphoreType.DMA
    args = [
        pltpu.with_memory_space_constraint(v, pltpu.HBM)
        for v in (latents, cotangent, chosen.reshape(1, T), codebook)
    ]
    gathered, code_grad = pl.pallas_call(
        kernel,
        out_shape=(pltpu.VMEM((PLANE, 16, 128), BF16), pltpu.VMEM((HALF, D), F32)),
        in_specs=[any_space] * 4,
        out_specs=(vmem, vmem),
        scratch_shapes=[
            pltpu.VMEM((CODES, D), BF16),
            pltpu.VMEM((NX, T, D), BF16),
            pltpu.VMEM((NX, T, D), BF16),
            pltpu.VMEM((NX, 1, T), jnp.int32),
            pltpu.VMEM((CODES, T), F32),
            pltpu.VMEM((CODES, T), F32),
            pltpu.VMEM((NX - 1, OWN, T), F32),
            pltpu.VMEM((NX - 1, OWN, T), F32),
            pltpu.VMEM((PLANE, 2, 2, 128), F32),
            pltpu.VMEM((NX, 2, 2, 128), F32),
            pltpu.VMEM((D, T), F32),
            pltpu.VMEM((D, T), F32),
            pltpu.VMEM((PLANE, 2, 16, 128), BF16),
            pltpu.VMEM((PLANE, 2, 16, 128), BF16),
            pltpu.VMEM((PLANE, 2, 2, 128), F32),
            pltpu.VMEM((16, 128), BF16),
            pltpu.VMEM((OWN, D), F32),
            pltpu.VMEM((HALF, D), BF16),
            pltpu.VMEM((HALF, D), BF16),
            dma((len(PARTS),)),
            dma((4,)),
            dma((3,)), dma((3,)),
            dma, dma,
            dma, dma,
            dma, dma,
            dma, dma,
            dma, dma,
            pltpu.SemaphoreType.REGULAR,
        ],
        compiler_params=pltpu.CompilerParams(
            collective_id=0, has_side_effects=True, vmem_limit_bytes=42 * 2**20
        ),
        cost_estimate=pl.CostEstimate(
            flops=20 * T * D * CODES, bytes_accessed=8 * 2**20, transcendentals=2 * T * CODES
        ),
    )(*args)
    return pl.pallas_call(
        finish,
        out_shape=(jax.ShapeDtypeStruct((T, D), F32), jax.ShapeDtypeStruct((HALF, D), F32)),
        in_specs=[vmem, vmem],
        out_specs=(any_space, any_space),
        scratch_shapes=[pltpu.VMEM((T, D), F32), dma((2,))],
        compiler_params=pltpu.CompilerParams(vmem_limit_bytes=4 * 2**20),
    )(*[pltpu.with_memory_space_constraint(v, pltpu.VMEM) for v in (gathered, code_grad)])


def solution(mesh):
    in_specs = (P("tok", None), P("code", None), P("tok", None), P("tok"))
    out_specs = (P("tok", None), P(("code", "tok"), None))
    return jax.shard_map(shards, mesh=mesh, in_specs=in_specs, out_specs=out_specs, check_vma=False)
```

```python
import jax
import jax.numpy as jnp
from jax import lax
from jax.experimental import pallas as pl
from jax.experimental.pallas import tpu as pltpu
from jax.sharding import PartitionSpec as P

MESH = pl.DeviceIdType.MESH
F32, BF16 = jnp.float32, jnp.bfloat16
NX, NY, NZ = 4, 4, 8
PLANE = NY * NZ
T = 256
D = 256
CODES = 8192
OWN = CODES // NX
HALF = OWN // 2
ROWS = 256

SHIFTS = sorted(
    ((dy, dz) for dy in range(NY) for dz in range(NZ) if (dy, dz) != (0, 0)),
    key=lambda s: (-min(s[1], NZ - s[1]), -min(s[0], NY - s[0])),
)
LOG2E = 1.4426950408889634
PARTS = (1024, 3072, 4096)
HALF_STEP = 512
STEP = 1024


def nt(a, b):
    return lax.dot_general(a, b, (((1,), (1,)), ((), ())), preferred_element_type=F32)


def tn(a, b):
    return lax.dot_general(a, b, (((0,), (0,)), ((), ())), preferred_element_type=F32)


def nn(a, b):
    return jnp.dot(a, b, preferred_element_type=F32)


def row(v):
    return jnp.concatenate([v[0:1], v[1:2]], axis=1)


def pair(v):
    return jnp.concatenate([v[:, :128], v[:, 128:]], axis=0)


def chunks(v):
    return jnp.concatenate(
        [v[:, :128].reshape(PLANE, 8, 128), v[:, 128:].reshape(PLANE, 8, 128)], axis=1
    ).astype(BF16)


def fold8(v):
    return v.reshape(v.shape[0] // 8, 8, v.shape[1])


def rank_of(y, z):
    late = jnp.where(z < 5, z, jnp.where(z == 7, 5, z + 1))
    return late * NY + y


def code_of(rank):
    y, late = rank & (NY - 1), rank >> 2
    z = jnp.where(late < 5, late, jnp.where(late == 5, 7, late - 1))
    return y * NZ + z


def kernel(
    lat_hbm, cot_hbm, cho_hbm, cb_hbm, ag, cg,
    cb, lat, cot, cho, lq, uu, lb, ub, stats, fin, acc_a, acc_b,
    rs_out, rs_in, coef, ag_own, cacc, cx_out, cx_in,
    cb_sem, own_sem, gat_send, gat_recv, st_send, st_recv, fin_send, fin_recv,
    rs_send, rs_recv, ag_send, ag_recv, cx_send, cx_recv, ready_sem, far_sem,
):
    tok, code = lax.axis_index("tok"), lax.axis_index("code")
    x, c = tok >> 1, tok & 1
    y, z = code >> 3, code & (NZ - 1)

    x_peers = [((((x + d) & (NX - 1)) << 1) + c, code) for d in range(1, NX)]
    x_right, x_left = x_peers[0], x_peers[2]
    plane_codes = [(((y + dy) & (NY - 1)) << 3) + ((z + dz) & (NZ - 1)) for dy, dz in SHIFTS]
    plane = [(tok, p) for p in plane_codes]
    other = (tok ^ 1, code)

    def remote(src, dst, send, recv, to):
        return pltpu.make_async_remote_copy(
            src_ref=src, dst_ref=dst, send_sem=send, recv_sem=recv, device_id=to, device_id_type=MESH
        )

    def all_of(ref, send, recv):
        return remote(ref, ref, send, recv, other)

    own = [
        pltpu.make_async_copy(lat_hbm, lat.at[0], own_sem.at[0]),
        pltpu.make_async_copy(cot_hbm, cot.at[0], own_sem.at[1]),
        pltpu.make_async_copy(cho_hbm, cho.at[0], own_sem.at[2]),
    ]
    starts = [sum(PARTS[:k]) for k in range(len(PARTS))]
    loads = [
        pltpu.make_async_copy(cb_hbm.at[pl.ds(at, n)], cb.at[pl.ds(at, n)], cb_sem.at[k])
        for k, (at, n) in enumerate(zip(starts, PARTS))
    ]
    own[0].start()
    for load in loads:
        load.start()
    own[1].start()
    own[2].start()

    rank = rank_of(y, z)

    def tell(sem):
        def one(r, carry):
            pl.semaphore_signal(sem, inc=1, device_id=(tok, code_of(r)), device_id_type=MESH)
            return carry

        return one

    with jax.named_scope("greet"):
        barrier = pltpu.get_barrier_semaphore()
        near = [x_right, x_left, other]
        for p in near:
            pl.semaphore_signal(barrier, inc=1, device_id=p, device_id_type=MESH)
        lax.fori_loop(rank + 1, PLANE, tell(barrier), 0)

    def logits(k, top):
        loads[k].wait()

        def step(j, top):
            for i in range(2):
                rows = pl.ds(pl.multiple_of(starts[k] + j * STEP + i * HALF_STEP, HALF_STEP), HALF_STEP)
                scores = nt(cb[rows, :], lat[0]) * LOG2E
                lq[rows, :] = scores
                top = jnp.maximum(top, jnp.max(fold8(scores), axis=0))
            return top

        return lax.fori_loop(0, PARTS[k] // STEP, step, top, unroll=True)

    with jax.named_scope("own_wait"):
        own[0].wait()
    with jax.named_scope("logits_first"):
        top8 = logits(0, jnp.full((8, T), -jnp.inf, F32))
        top8 = logits(1, top8)

    with jax.named_scope("entry"):
        pl.semaphore_wait(barrier, len(near) + rank)
    arrays = ((lat_hbm, lat), (cot_hbm, cot), (cho_hbm, cho))
    to_right = [remote(v, w.at[1], gat_send.at[i], gat_recv.at[i], x_right) for i, (v, w) in enumerate(arrays)]
    to_left = [remote(v, w.at[3], gat_send.at[3 + i], gat_recv.at[3 + i], x_left) for i, (v, w) in enumerate(arrays)]
    passed = [
        remote(lat.at[1], lat.at[2], gat_send.at[6], gat_recv.at[6], x_right),
        remote(cot.at[3], cot.at[2], gat_send.at[7], gat_recv.at[7], x_left),
        remote(cho.at[3], cho.at[2], gat_send.at[8], gat_recv.at[8], x_left),
    ]
    for copy in (to_right[0], to_left[1], to_left[2], to_right[1], to_left[0], to_right[2]):
        copy.start()
    pl.semaphore_signal(far_sem, inc=1, device_id=x_right, device_id_type=MESH)
    lax.fori_loop(0, rank, tell(ready_sem), 0)
    late = z >= NZ // 2

    with jax.named_scope("logits_rest"):
        top8 = logits(2, top8)
        top = jnp.max(top8, axis=0, keepdims=True)
        own[1].wait()
        own[2].wait()

    with jax.named_scope("stats"):

        def stats_step(k, carry):
            total8, inner8 = carry
            rows = pl.ds(pl.multiple_of(k * STEP, STEP), STEP)
            up = nt(cb[rows, :], cot[0])
            uu[rows, :] = up
            q = jnp.exp2(lq[rows, :] - top)
            lq[rows, :] = q
            total8 = total8 + jnp.sum(fold8(q), axis=0)
            inner8 = inner8 + jnp.sum(fold8(q * up), axis=0)
            return total8, inner8

        zero8 = jnp.zeros((8, T), F32)
        total8, inner8 = lax.fori_loop(0, CODES // STEP, stats_step, (zero8, zero8), unroll=True)
        total = jnp.sum(total8, axis=0, keepdims=True)
        inner = jnp.sum(inner8, axis=0, keepdims=True)
        inner_loc = inner / total
        stats[0, 0] = pair(top + jnp.log(total) * LOG2E)
        stats[0, 1] = pair(inner_loc)

    def send_stats():
        with jax.named_scope("ready"):

            @pl.when(rank < PLANE - 1)
            def later_ones():
                pl.semaphore_wait(ready_sem, PLANE - 1 - rank)

        for k, p in enumerate(plane):
            remote(stats.at[0], stats.at[k + 1], st_send, st_recv, p).start()

    pl.when(late)(send_stats)

    with jax.named_scope("sums"):
        acc_a[...] = jnp.zeros_like(acc_a)
        acc_b[...] = jnp.zeros_like(acc_b)

        def sums_step(k, carry):
            rows = pl.ds(pl.multiple_of(k * STEP, STEP), STEP)
            q = lq[rows, :]
            part = cb[rows, :]
            acc_a[...] += tn(part, (q * (uu[rows, :] - inner_loc)).astype(BF16))
            acc_b[...] += tn(part, q.astype(BF16))
            return carry

        lax.fori_loop(0, CODES // STEP, sums_step, 0, unroll=True)
        for i, acc in enumerate((acc_a, acc_b)):
            rs_out[:, i] = chunks(acc[...] * (1.0 / total))
    pl.when(jnp.logical_not(late))(send_stats)
    for k, p in enumerate(plane):
        remote(rs_out.at[plane_codes[k]], rs_in.at[k + 1], rs_send, rs_recv, p).start()
    rs_local = pltpu.make_async_copy(rs_out.at[code], rs_in.at[0], own_sem.at[3])
    rs_local.start()
    with jax.named_scope("forward"):
        to_right[0].wait_recv()
        passed[0].start()
        to_left[1].wait_recv()
        passed[1].start()
        to_left[2].wait_recv()
        passed[2].start()

    with jax.named_scope("stats_wait"):
        all_of(stats.at[pl.ds(1, PLANE - 1)], st_send, st_recv).wait_recv()
    with jax.named_scope("combine"):
        logs = stats[:, 0]
        inners = stats[:, 1]
        big = jnp.max(logs, axis=0)
        weights = jnp.exp2(logs - big)
        whole = jnp.sum(weights, axis=0)
        weights = weights * (1.0 / whole)
        mean = jnp.sum(weights * inners, axis=0)
        fin[0, 0] = big + jnp.log(whole) * LOG2E
        fin[0, 1] = mean
        coef[:, 0] = weights
        coef[:, 1] = weights * (mean - inners)
        own_scale = row(weights[0]) * (1.0 / total)
        own_inner = row(mean)
    with jax.named_scope("far"):
        pl.semaphore_wait(far_sem, 1)
    for d in (2, 1, 3):
        remote(fin.at[0], fin.at[d], fin_send, fin_recv, x_peers[d - 1]).start()

    base = pl.multiple_of(x * OWN, OWN)

    def scores_of_codes():
        with jax.named_scope("gather_wait"):
            for copy in to_left[:1] + to_right[1:] + passed:
                copy.wait_recv()
        with jax.named_scope("code_scores"):
            codes = pl.ds(base, OWN)
            for g in range(1, NX):
                lb[g - 1] = nt(cb[codes, :], lat[g]) * LOG2E
                ub[g - 1] = nt(cb[codes, :], cot[g])
        with jax.named_scope("chosen"):
            ids = lax.broadcasted_iota(jnp.int32, (ROWS, T), 0)
            all_cot = cot[...].reshape(NX * T, D)

            def chosen_step(k, carry):
                at = pl.multiple_of(k * ROWS, ROWS)
                first = code * CODES + base + at
                hot = [jnp.where(ids == cho[g] - first, 1.0, 0.0).astype(BF16) for g in range(NX)]
                cacc[pl.ds(at, ROWS), :] = nn(jnp.concatenate(hot, axis=1), all_cot)
                return carry

            lax.fori_loop(0, OWN // ROWS, chosen_step, 0, unroll=True)

    pl.when(z < 2)(scores_of_codes)

    with jax.named_scope("rs_wait"):
        rs_local.wait()
        all_of(rs_in.at[pl.ds(1, PLANE - 1)], rs_send, rs_recv).wait_recv()
    with jax.named_scope("latent_sum"):
        parts = rs_in[...].astype(F32).reshape(PLANE, 2, 2, 8, 128)
        by_a = coef[:, 0].reshape(PLANE, 2, 1, 128)
        by_b = coef[:, 1].reshape(PLANE, 2, 1, 128)
        mine = jnp.sum(by_a * parts[:, 0] - by_b * parts[:, 1], axis=0)
        ag_own[...] = mine.reshape(16, 128).astype(BF16)
        ag[code] = ag_own[...]

    def ag_to(r, carry):
        remote(ag_own, ag.at[code], ag_send, ag_recv, (tok, code_of(r))).start()
        return carry

    lax.fori_loop(0, rank, ag_to, 0)
    lax.fori_loop(rank + 1, PLANE, ag_to, 0)

    pl.when(z >= 2)(scores_of_codes)

    with jax.named_scope("fin_wait"):
        all_of(fin.at[pl.ds(1, NX - 1)], fin_send, fin_recv).wait_recv()

    with jax.named_scope("code_grads"):
        logs_of = [row(fin[g, 0]) for g in range(NX)]
        means = [row(fin[g, 1]) for g in range(NX)]
        all_lat = lat[...].reshape(NX * T, D)

        def grads_of(half, k):
            at = pl.multiple_of(half * HALF + k * ROWS, ROWS)
            rows = pl.ds(at, ROWS)
            own_rows = pl.ds(pl.multiple_of(base + at, ROWS), ROWS)
            dlogits = [((lq[own_rows, :] * own_scale) * (uu[own_rows, :] - own_inner)).astype(BF16)]
            for g in range(1, NX):
                probs = jnp.exp2(lb[g - 1, rows, :] - logs_of[g])
                dlogits.append((probs * (ub[g - 1, rows, :] - means[g])).astype(BF16))
            return cacc[rows, :] + nn(jnp.concatenate(dlogits, axis=1), all_lat)

        def other_step(k, carry):
            cx_out[pl.ds(pl.multiple_of(k * ROWS, ROWS), ROWS), :] = grads_of(1 - c, k).astype(BF16)
            return carry

        lax.fori_loop(0, HALF // ROWS, other_step, 0, unroll=True)
        to_other = remote(cx_out, cx_in, cx_send, cx_recv, other)
        to_other.start()

        def own_step(k, carry):
            cg[pl.ds(pl.multiple_of(k * ROWS, ROWS), ROWS), :] = grads_of(c, k)
            return carry

        lax.fori_loop(0, HALF // ROWS, own_step, 0, unroll=True)

    with jax.named_scope("core_wait"):
        to_other.wait_recv()
    with jax.named_scope("code_out"):
        cg[...] += cx_in[...].astype(F32)

    with jax.named_scope("drain"):
        to_other.wait_send()
        for copy in to_right + to_left + passed:
            copy.wait_send()
        all_of(stats.at[pl.ds(1, PLANE - 1)], st_send, st_recv).wait_send()
        all_of(fin.at[pl.ds(1, NX - 1)], fin_send, fin_recv).wait_send()
        all_of(rs_in.at[pl.ds(1, PLANE - 1)], rs_send, rs_recv).wait_send()

    with jax.named_scope("ag_wait"):
        all_of(ag.at[pl.ds(0, PLANE - 1)], ag_send, ag_recv).wait_send()
        all_of(ag.at[pl.ds(0, PLANE - 1)], ag_send, ag_recv).wait_recv()


def finish(ag, cg, lg_out, cg_out, lg_v, sem):
    move = pltpu.make_async_copy(cg, cg_out, sem.at[0])
    move.start()
    full = ag[...].astype(F32)
    lg_v[pl.ds(0, 128), :] = full[:, :8, :].reshape(D, 128).T
    lg_v[pl.ds(128, 128), :] = full[:, 8:, :].reshape(D, 128).T
    store = pltpu.make_async_copy(lg_v, lg_out, sem.at[1])
    store.start()
    with jax.named_scope("store_latent"):
        store.wait()
    with jax.named_scope("store_code"):
        move.wait()


def shards(latents, codebook, cotangent, chosen):
    any_space = pl.BlockSpec(memory_space=pl.ANY)
    vmem = pl.BlockSpec(memory_space=pltpu.VMEM)
    dma = pltpu.SemaphoreType.DMA
    args = [
        pltpu.with_memory_space_constraint(v, pltpu.HBM)
        for v in (latents, cotangent, chosen.reshape(1, T), codebook)
    ]
    gathered, code_grad = pl.pallas_call(
        kernel,
        out_shape=(pltpu.VMEM((PLANE, 16, 128), BF16), pltpu.VMEM((HALF, D), F32)),
        in_specs=[any_space] * 4,
        out_specs=(vmem, vmem),
        scratch_shapes=[
            pltpu.VMEM((CODES, D), BF16),
            pltpu.VMEM((NX, T, D), BF16),
            pltpu.VMEM((NX, T, D), BF16),
            pltpu.VMEM((NX, 1, T), jnp.int32),
            pltpu.VMEM((CODES, T), F32),
            pltpu.VMEM((CODES, T), F32),
            pltpu.VMEM((NX - 1, OWN, T), F32),
            pltpu.VMEM((NX - 1, OWN, T), F32),
            pltpu.VMEM((PLANE, 2, 2, 128), F32),
            pltpu.VMEM((NX, 2, 2, 128), F32),
            pltpu.VMEM((D, T), F32),
            pltpu.VMEM((D, T), F32),
            pltpu.VMEM((PLANE, 2, 16, 128), BF16),
            pltpu.VMEM((PLANE, 2, 16, 128), BF16),
            pltpu.VMEM((PLANE, 2, 2, 128), F32),
            pltpu.VMEM((16, 128), BF16),
            pltpu.VMEM((OWN, D), F32),
            pltpu.VMEM((HALF, D), BF16),
            pltpu.VMEM((HALF, D), BF16),
            dma((len(PARTS),)),
            dma((4,)),
            dma((9,)), dma((9,)),
            dma, dma,
            dma, dma,
            dma, dma,
            dma, dma,
            dma, dma,
            pltpu.SemaphoreType.REGULAR,
            pltpu.SemaphoreType.REGULAR,
        ],
        compiler_params=pltpu.CompilerParams(
            collective_id=0, has_side_effects=True, vmem_limit_bytes=42 * 2**20
        ),
        cost_estimate=pl.CostEstimate(
            flops=20 * T * D * CODES, bytes_accessed=8 * 2**20, transcendentals=2 * T * CODES
        ),
    )(*args)
    return pl.pallas_call(
        finish,
        out_shape=(jax.ShapeDtypeStruct((T, D), F32), jax.ShapeDtypeStruct((HALF, D), F32)),
        in_specs=[vmem, vmem],
        out_specs=(any_space, any_space),
        scratch_shapes=[pltpu.VMEM((T, D), F32), dma((2,))],
        compiler_params=pltpu.CompilerParams(vmem_limit_bytes=4 * 2**20),
    )(*[pltpu.with_memory_space_constraint(v, pltpu.VMEM) for v in (gathered, code_grad)])


def solution(mesh):
    in_specs = (P("tok", None), P("code", None), P("tok", None), P("tok"))
    out_specs = (P("tok", None), P(("code", "tok"), None))
    return jax.shard_map(shards, mesh=mesh, in_specs=in_specs, out_specs=out_specs, check_vma=False)
```

```python
import jax
import jax.numpy as jnp
from jax import lax
from jax.experimental import pallas as pl
from jax.experimental.pallas import tpu as pltpu
from jax.sharding import PartitionSpec as P

MESH = pl.DeviceIdType.MESH
F32, BF16 = jnp.float32, jnp.bfloat16
NX, NY, NZ = 4, 4, 8
PLANE = NY * NZ
T = 256
D = 256
CODES = 8192
OWN = CODES // NX
HALF = OWN // 2
ROWS = 256

SHIFTS = sorted(
    ((dy, dz) for dy in range(NY) for dz in range(NZ) if (dy, dz) != (0, 0)),
    key=lambda s: -(min(s[0], NY - s[0]) + min(s[1], NZ - s[1])),
)
LOG2E = 1.4426950408889634
PARTS = (1024, 3072, 4096)
STEP = 1024


def nt(a, b):
    return lax.dot_general(a, b, (((1,), (1,)), ((), ())), preferred_element_type=F32)


def tn(a, b):
    return lax.dot_general(a, b, (((0,), (0,)), ((), ())), preferred_element_type=F32)


def nn(a, b):
    return jnp.dot(a, b, preferred_element_type=F32)


def row(v):
    return jnp.concatenate([v[0:1], v[1:2]], axis=1)


def pair(v):
    return jnp.concatenate([v[:, :128], v[:, 128:]], axis=0)


def fold8(v):
    return v.reshape(v.shape[0] // 8, 8, v.shape[1])


def rank_of(y, z):
    late = jnp.where(z < 5, z, jnp.where(z == 7, 5, z + 1))
    return late * NY + y


def code_of(rank):
    y, late = rank & (NY - 1), rank >> 2
    z = jnp.where(late < 5, late, jnp.where(late == 5, 7, late - 1))
    return y * NZ + z


def kernel(
    lat_hbm, cot_hbm, cho_hbm, cb_hbm, ag, cg,
    cb, lat, cot, cho, lq, uu, lb, ub, stats, fin, acc_a, acc_b,
    rs_out, rs_in, coef, ag_own, cacc, cx_out, cx_in,
    cb_sem, own_sem, gat_send, gat_recv, st_send, st_recv, fin_send, fin_recv,
    rs_send, rs_recv, ag_send, ag_recv, cx_send, cx_recv, ready_sem,
):
    tok, code = lax.axis_index("tok"), lax.axis_index("code")
    x, c = tok >> 1, tok & 1
    y, z = code >> 3, code & (NZ - 1)

    x_peers = [((((x + d) & (NX - 1)) << 1) + c, code) for d in range(1, NX)]
    plane_codes = [(((y + dy) & (NY - 1)) << 3) + ((z + dz) & (NZ - 1)) for dy, dz in SHIFTS]
    plane = [(tok, p) for p in plane_codes]
    other = (tok ^ 1, code)

    def remote(src, dst, send, recv, to):
        return pltpu.make_async_remote_copy(
            src_ref=src, dst_ref=dst, send_sem=send, recv_sem=recv, device_id=to, device_id_type=MESH
        )

    def all_of(ref, send, recv):
        return remote(ref, ref, send, recv, other)

    own = [
        pltpu.make_async_copy(lat_hbm, lat.at[0], own_sem.at[0]),
        pltpu.make_async_copy(cot_hbm, cot.at[0], own_sem.at[1]),
        pltpu.make_async_copy(cho_hbm, cho.at[0], own_sem.at[2]),
    ]
    starts = [sum(PARTS[:k]) for k in range(len(PARTS))]
    loads = [
        pltpu.make_async_copy(cb_hbm.at[pl.ds(at, n)], cb.at[pl.ds(at, n)], cb_sem.at[k])
        for k, (at, n) in enumerate(zip(starts, PARTS))
    ]
    own[0].start()
    for load in loads:
        load.start()
    own[1].start()
    own[2].start()

    rank = rank_of(y, z)

    def tell(sem):
        def one(r, carry):
            pl.semaphore_signal(sem, inc=1, device_id=(tok, code_of(r)), device_id_type=MESH)
            return carry

        return one

    with jax.named_scope("greet"):
        barrier = pltpu.get_barrier_semaphore()
        near = x_peers + [other]
        for p in near:
            pl.semaphore_signal(barrier, inc=1, device_id=p, device_id_type=MESH)
        lax.fori_loop(rank + 1, PLANE, tell(barrier), 0)

    def logits(k, top):
        loads[k].wait()

        def step(j, top):
            rows = pl.ds(pl.multiple_of(starts[k] + j * STEP, STEP), STEP)
            scores = nt(cb[rows, :], lat[0]) * LOG2E
            lq[rows, :] = scores
            return jnp.maximum(top, jnp.max(fold8(scores), axis=0))

        return lax.fori_loop(0, PARTS[k] // STEP, step, top, unroll=True)

    with jax.named_scope("own_wait"):
        own[0].wait()
    with jax.named_scope("logits_first"):
        top8 = logits(0, jnp.full((8, T), -jnp.inf, F32))
        top8 = logits(1, top8)

    with jax.named_scope("entry"):
        pl.semaphore_wait(barrier, len(near) + rank)
    for d in (2, 1, 3):
        to = x_peers[d - 1]
        remote(lat_hbm, lat.at[d], gat_send.at[0], gat_recv.at[0], to).start()
        remote(cot_hbm, cot.at[d], gat_send.at[1], gat_recv.at[1], to).start()
        remote(cho_hbm, cho.at[d], gat_send.at[2], gat_recv.at[2], to).start()
    lax.fori_loop(0, rank, tell(ready_sem), 0)

    with jax.named_scope("logits_rest"):
        top8 = logits(2, top8)
        top = jnp.max(top8, axis=0, keepdims=True)
        own[1].wait()
        own[2].wait()

    with jax.named_scope("stats"):

        def stats_step(k, carry):
            total8, inner8 = carry
            rows = pl.ds(pl.multiple_of(k * STEP, STEP), STEP)
            up = nt(cb[rows, :], cot[0])
            uu[rows, :] = up
            q = jnp.exp2(lq[rows, :] - top)
            lq[rows, :] = q
            total8 = total8 + jnp.sum(fold8(q), axis=0)
            inner8 = inner8 + jnp.sum(fold8(q * up), axis=0)
            return total8, inner8

        zero8 = jnp.zeros((8, T), F32)
        total8, inner8 = lax.fori_loop(0, CODES // STEP, stats_step, (zero8, zero8), unroll=True)
        total = jnp.sum(total8, axis=0, keepdims=True)
        inner = jnp.sum(inner8, axis=0, keepdims=True)
        inner_loc = inner / total
        stats[0, 0] = pair(top + jnp.log(total) * LOG2E)
        stats[0, 1] = pair(inner_loc)

    def send_stats():
        with jax.named_scope("ready"):

            @pl.when(rank < PLANE - 1)
            def later_ones():
                pl.semaphore_wait(ready_sem, PLANE - 1 - rank)

        for k, p in enumerate(plane):
            remote(stats.at[0], stats.at[k + 1], st_send, st_recv, p).start()

    pl.when(z >= NZ // 2)(send_stats)

    with jax.named_scope("sums"):
        acc_a[...] = jnp.zeros_like(acc_a)
        acc_b[...] = jnp.zeros_like(acc_b)

        def sums_step(k, carry):
            rows = pl.ds(pl.multiple_of(k * STEP, STEP), STEP)
            q = lq[rows, :]
            part = cb[rows, :]
            acc_a[...] += tn(part, (q * (uu[rows, :] - inner_loc)).astype(BF16))
            acc_b[...] += tn(part, q.astype(BF16))
            return carry

        lax.fori_loop(0, CODES // STEP, sums_step, 0, unroll=True)

        for i, acc in enumerate((acc_a, acc_b)):
            whole = acc[...] * (1.0 / total)
            rs_out[:, i] = jnp.concatenate(
                [whole[:, :128].reshape(PLANE, 8, 128), whole[:, 128:].reshape(PLANE, 8, 128)], axis=1
            ).astype(BF16)
    pl.when(z < NZ // 2)(send_stats)
    for k, p in enumerate(plane):
        remote(rs_out.at[plane_codes[k]], rs_in.at[k + 1], rs_send, rs_recv, p).start()
    rs_local = pltpu.make_async_copy(rs_out.at[code], rs_in.at[0], own_sem.at[3])
    rs_local.start()

    with jax.named_scope("stats_wait"):
        all_of(stats.at[pl.ds(1, PLANE - 1)], st_send, st_recv).wait_recv()
    with jax.named_scope("combine"):
        logs = stats[:, 0]
        inners = stats[:, 1]
        big = jnp.max(logs, axis=0)
        weights = jnp.exp2(logs - big)
        whole = jnp.sum(weights, axis=0)
        weights = weights * (1.0 / whole)
        mean = jnp.sum(weights * inners, axis=0)
        fin[0, 0] = big + jnp.log(whole) * LOG2E
        fin[0, 1] = mean
        coef[:, 0] = weights
        coef[:, 1] = weights * (mean - inners)
        own_scale = row(weights[0]) * (1.0 / total)
        own_inner = row(mean)
    for d in (2, 1, 3):
        remote(fin.at[0], fin.at[d], fin_send, fin_recv, x_peers[d - 1]).start()

    base = pl.multiple_of(x * OWN, OWN)

    def scores_of_codes():
        with jax.named_scope("gather_wait"):
            all_of(lat.at[pl.ds(1, NX - 1)], gat_send.at[0], gat_recv.at[0]).wait_recv()
            all_of(cot.at[pl.ds(1, NX - 1)], gat_send.at[1], gat_recv.at[1]).wait_recv()
            all_of(cho.at[pl.ds(1, NX - 1)], gat_send.at[2], gat_recv.at[2]).wait_recv()
        with jax.named_scope("code_scores"):
            codes = pl.ds(base, OWN)
            for g in range(1, NX):
                lb[g - 1] = nt(cb[codes, :], lat[g]) * LOG2E
                ub[g - 1] = nt(cb[codes, :], cot[g])
        with jax.named_scope("chosen"):
            ids = lax.broadcasted_iota(jnp.int32, (ROWS, T), 0)
            all_cot = cot[...].reshape(NX * T, D)

            def chosen_step(k, carry):
                at = pl.multiple_of(k * ROWS, ROWS)
                first = code * CODES + base + at
                hot = [jnp.where(ids == cho[g] - first, 1.0, 0.0).astype(BF16) for g in range(NX)]
                cacc[pl.ds(at, ROWS), :] = nn(jnp.concatenate(hot, axis=1), all_cot)
                return carry

            lax.fori_loop(0, OWN // ROWS, chosen_step, 0, unroll=True)

    pl.when(z < NZ // 2 - 1)(scores_of_codes)

    with jax.named_scope("rs_wait"):
        rs_local.wait()
        all_of(rs_in.at[pl.ds(1, PLANE - 1)], rs_send, rs_recv).wait_recv()
    with jax.named_scope("latent_sum"):
        parts = rs_in[...].astype(F32).reshape(PLANE, 2, 2, 8, 128)
        by_a = coef[:, 0].reshape(PLANE, 2, 1, 128)
        by_b = coef[:, 1].reshape(PLANE, 2, 1, 128)
        mine = jnp.sum(by_a * parts[:, 0] - by_b * parts[:, 1], axis=0)
        ag_own[...] = mine.reshape(16, 128).astype(BF16)
        ag[code] = ag_own[...]

    def ag_to(r, carry):
        remote(ag_own, ag.at[code], ag_send, ag_recv, (tok, code_of(r))).start()
        return carry

    lax.fori_loop(0, rank, ag_to, 0)
    lax.fori_loop(rank + 1, PLANE, ag_to, 0)

    pl.when(z >= NZ // 2 - 1)(scores_of_codes)

    with jax.named_scope("fin_wait"):
        all_of(fin.at[pl.ds(1, NX - 1)], fin_send, fin_recv).wait_recv()

    with jax.named_scope("code_grads"):
        logs_of = [row(fin[g, 0]) for g in range(NX)]
        means = [row(fin[g, 1]) for g in range(NX)]
        all_lat = lat[...].reshape(NX * T, D)

        def grads_of(half, k):
            at = pl.multiple_of(half * HALF + k * ROWS, ROWS)
            rows = pl.ds(at, ROWS)
            own_rows = pl.ds(pl.multiple_of(base + at, ROWS), ROWS)
            dlogits = [((lq[own_rows, :] * own_scale) * (uu[own_rows, :] - own_inner)).astype(BF16)]
            for g in range(1, NX):
                probs = jnp.exp2(lb[g - 1, rows, :] - logs_of[g])
                dlogits.append((probs * (ub[g - 1, rows, :] - means[g])).astype(BF16))
            return cacc[rows, :] + nn(jnp.concatenate(dlogits, axis=1), all_lat)

        def other_step(k, carry):
            cx_out[pl.ds(pl.multiple_of(k * ROWS, ROWS), ROWS), :] = grads_of(1 - c, k).astype(BF16)
            return carry

        lax.fori_loop(0, HALF // ROWS, other_step, 0, unroll=True)
        to_other = remote(cx_out, cx_in, cx_send, cx_recv, other)
        to_other.start()

        def own_step(k, carry):
            cg[pl.ds(pl.multiple_of(k * ROWS, ROWS), ROWS), :] = grads_of(c, k)
            return carry

        lax.fori_loop(0, HALF // ROWS, own_step, 0, unroll=True)

    with jax.named_scope("core_wait"):
        to_other.wait_recv()
    with jax.named_scope("code_out"):
        cg[...] += cx_in[...].astype(F32)

    with jax.named_scope("drain"):
        to_other.wait_send()
        all_of(lat.at[pl.ds(1, NX - 1)], gat_send.at[0], gat_recv.at[0]).wait_send()
        all_of(cot.at[pl.ds(1, NX - 1)], gat_send.at[1], gat_recv.at[1]).wait_send()
        all_of(cho.at[pl.ds(1, NX - 1)], gat_send.at[2], gat_recv.at[2]).wait_send()
        all_of(stats.at[pl.ds(1, PLANE - 1)], st_send, st_recv).wait_send()
        all_of(fin.at[pl.ds(1, NX - 1)], fin_send, fin_recv).wait_send()
        all_of(rs_in.at[pl.ds(1, PLANE - 1)], rs_send, rs_recv).wait_send()

    with jax.named_scope("ag_wait"):
        all_of(ag.at[pl.ds(0, PLANE - 1)], ag_send, ag_recv).wait_send()
        all_of(ag.at[pl.ds(0, PLANE - 1)], ag_send, ag_recv).wait_recv()


def finish(ag, cg, lg_out, cg_out, lg_v, sem):
    moves = []
    for k in range(8):
        piece = pl.ds(k * (HALF // 8), HALF // 8)
        moves.append(pltpu.make_async_copy(cg.at[piece], cg_out.at[piece], sem.at[k]))
        moves[-1].start()
    full = ag[...].astype(F32)
    for k in range(2):
        piece = pl.ds(k * 128, 128)
        lg_v[piece, :] = full[:, k * 8 : k * 8 + 8, :].reshape(D, 128).T
        moves.append(pltpu.make_async_copy(lg_v.at[piece], lg_out.at[piece], sem.at[8 + k]))
        moves[-1].start()
    with jax.named_scope("stores"):
        for move in moves:
            move.wait()


def shards(latents, codebook, cotangent, chosen):
    any_space = pl.BlockSpec(memory_space=pl.ANY)
    vmem = pl.BlockSpec(memory_space=pltpu.VMEM)
    dma = pltpu.SemaphoreType.DMA
    args = [
        pltpu.with_memory_space_constraint(v, pltpu.HBM)
        for v in (latents, cotangent, chosen.reshape(1, T), codebook)
    ]
    gathered, code_grad = pl.pallas_call(
        kernel,
        out_shape=(pltpu.VMEM((PLANE, 16, 128), BF16), pltpu.VMEM((HALF, D), F32)),
        in_specs=[any_space] * 4,
        out_specs=(vmem, vmem),
        scratch_shapes=[
            pltpu.VMEM((CODES, D), BF16),
            pltpu.VMEM((NX, T, D), BF16),
            pltpu.VMEM((NX, T, D), BF16),
            pltpu.VMEM((NX, 1, T), jnp.int32),
            pltpu.VMEM((CODES, T), F32),
            pltpu.VMEM((CODES, T), F32),
            pltpu.VMEM((NX - 1, OWN, T), F32),
            pltpu.VMEM((NX - 1, OWN, T), F32),
            pltpu.VMEM((PLANE, 2, 2, 128), F32),
            pltpu.VMEM((NX, 2, 2, 128), F32),
            pltpu.VMEM((D, T), F32),
            pltpu.VMEM((D, T), F32),
            pltpu.VMEM((PLANE, 2, 16, 128), BF16),
            pltpu.VMEM((PLANE, 2, 16, 128), BF16),
            pltpu.VMEM((PLANE, 2, 2, 128), F32),
            pltpu.VMEM((16, 128), BF16),
            pltpu.VMEM((OWN, D), F32),
            pltpu.VMEM((HALF, D), BF16),
            pltpu.VMEM((HALF, D), BF16),
            dma((len(PARTS),)),
            dma((4,)),
            dma((3,)), dma((3,)),
            dma, dma,
            dma, dma,
            dma, dma,
            dma, dma,
            dma, dma,
            pltpu.SemaphoreType.REGULAR,
        ],
        compiler_params=pltpu.CompilerParams(
            collective_id=0, has_side_effects=True, vmem_limit_bytes=42 * 2**20
        ),
        cost_estimate=pl.CostEstimate(
            flops=20 * T * D * CODES, bytes_accessed=8 * 2**20, transcendentals=2 * T * CODES
        ),
    )(*args)
    return pl.pallas_call(
        finish,
        out_shape=(jax.ShapeDtypeStruct((T, D), F32), jax.ShapeDtypeStruct((HALF, D), F32)),
        in_specs=[vmem, vmem],
        out_specs=(any_space, any_space),
        scratch_shapes=[pltpu.VMEM((T, D), F32), dma((10,))],
        compiler_params=pltpu.CompilerParams(vmem_limit_bytes=4 * 2**20),
    )(*[pltpu.with_memory_space_constraint(v, pltpu.VMEM) for v in (gathered, code_grad)])


def solution(mesh):
    in_specs = (P("tok", None), P("code", None), P("tok", None), P("tok"))
    out_specs = (P("tok", None), P(("code", "tok"), None))
    return jax.shard_map(shards, mesh=mesh, in_specs=in_specs, out_specs=out_specs, check_vma=False)
```
